32 devices in a mesh: group: 2 (over x), wide: 2 (over core), tensor: 8 (over z, y).
Axes of the slice: x: 2, y: 2, z: 4, core: 2. Of those that a mesh axis runs over, the one named last changes fastest.
Arguments:
- tokens: bfloat16 [512, 8192], P(('group', 'wide'), 'tensor'), parts along dimension 0, may hold values from -6 to 6
- gain: float32 [16384], P('group'), parts along dimension 0, may hold values from 0.5 to 2
- gate_weight: bfloat16 [16384, 16384], P(('group', 'wide', 'tensor')), parts along dimension 0, may hold values from -0.09375 to 0.09375
- up_weight: bfloat16 [16384, 16384], P(('group', 'wide', 'tensor')), parts along dimension 0, may hold values from -0.09375 to 0.09375
- gate_mask: int32 [256, 256], P('group'), parts along dimension 0, may hold values from 0 to 1, as said below
- up_mask: int32 [256, 256], P('group'), parts along dimension 0, may hold values from 0 to 1, as said below
Outputs:
- hidden: bfloat16 [512, 16384], P(('group', 'wide'), 'tensor'), parts along dimension 0
The draws below stay inside these ranges and needn't reach their ends.
There are 2 independent parts, one for each index of `group`. The reference program is written for one: setup_inputs(seed, part) draws one part's arguments, and reference() takes and returns one part's arrays. A program takes and returns all parts, laid end to end along the dimension named above; each array names one. Nothing has to cross between parts.
Inputs may be any that keep to these rules, and one draw needn't show every extreme that they name: `gate_mask`: A 1 keeps a block, a 0 prunes it; the share of kept blocks differs between groups of consecutive hidden-unit blocks. `up_mask`: as for gate_mask.
All inputs are finite; a program needn't handle non-finite values.
Results may differ from the reference program's by a relative error of at most 0.0058.
Values may be sent and summed in bfloat16 or wider, within the bound.
No kernel may reach another device: no remote copies, remote signals or barrier semaphores. Data moves between devices by JAX's collectives and lax.ppermute only.
A program may use at most 256 MiB of HBM per device.

```python
import math
import jax
import jax.numpy as jnp
from jax import lax

D = 8192
FF = 16384
BS = 64
TOKENS = 256
N_TENSOR = 8


def mask_draw(key, rows, cols, groups):
    first = jax.random.fold_in(key, 11)
    second = jax.random.fold_in(key, 23)
    levels = jax.random.randint(first, (groups,), 1, 4)
    limits = jnp.repeat(levels, cols // groups)[None, :]
    draws = jax.random.randint(second, (rows, cols), 0, 4)
    return (draws < limits).astype(jnp.int32)


def draw_gate_mask(key, part):
    return mask_draw(jax.random.fold_in(key, 1), D // BS, FF // BS, N_TENSOR)


def draw_up_mask(key, part):
    return mask_draw(jax.random.fold_in(key, 2), D // BS, FF // BS, N_TENSOR)


def steps_of(own_key, dims, shards, low, top_value):
    level = 1.0
    for axis_at, blocks in shards:
        heights = jax.random.uniform(jax.random.fold_in(jax.random.fold_in(own_key, 6), axis_at), (blocks,), jnp.float32, low / len(shards), top_value / len(shards))
        level = level * jnp.repeat(jnp.exp(heights), dims[axis_at] // blocks).reshape((-1,) + (1,) * (len(dims) - 1 - axis_at))
    return level


def normal_values(rng, dims, scale, limit, pieces=(), held_as=jnp.bfloat16):
    entries = scale * jax.random.normal(rng, dims, jnp.float32)
    if pieces:
        entries = entries * steps_of(rng, dims, pieces, -0.22, 0.18)
    return jnp.clip(entries, -limit, limit).astype(held_as)


def setup_inputs(seed: int = 0, part: int = 0) -> dict:
    seeds = jax.random.split(jax.random.key(seed), 7)
    own_keys = jax.random.split(jax.random.fold_in(seeds[6], part), 7)
    return {
        "tokens": normal_values(own_keys[0], (TOKENS, D), 1.0, 6.0, ((0, 2), (1, 8))),
        "gain": jnp.clip(jnp.exp(jax.random.uniform(own_keys[1], (D,), jnp.float32, math.log(0.5), math.log(2.0))), 0.5, 2.0),
        "gate_weight": normal_values(own_keys[2], (D, FF), (D // 2) ** -0.5, 0.09375, ((0, 16),)),
        "up_weight": normal_values(own_keys[3], (D, FF), (D // 2) ** -0.5, 0.09375, ((0, 16),)),
        "gate_mask": draw_gate_mask(jax.random.fold_in(jax.random.fold_in(seeds[6], part), 71), part),
        "up_mask": draw_up_mask(jax.random.fold_in(jax.random.fold_in(seeds[6], part), 71), part),
    }


def expand(mask, weight):
    rows, cols = mask.shape
    blocks = weight.reshape(rows, BS, cols, BS) * mask.astype(jnp.bfloat16)[:, None, :, None]
    return blocks.reshape(weight.shape)

def reference(tokens, gain, gate_weight, up_weight, gate_mask, up_mask):
    values = tokens.astype(jnp.float32)
    scale = lax.rsqrt(lax.optimization_barrier(jnp.mean(values * values, axis=-1, keepdims=True)) + 1e-05)
    normed = (values * scale * gain).astype(jnp.bfloat16)
    gate = jnp.dot(normed, expand(gate_mask, gate_weight), preferred_element_type=jnp.float32)
    up = jnp.dot(normed, expand(up_mask, up_weight), preferred_element_type=jnp.float32)
    return (jax.nn.silu(gate) * up).astype(jnp.bfloat16)
```

```python
import functools

import jax
import jax.numpy as jnp
from jax import lax
from jax.experimental import pallas as pl
from jax.experimental.pallas import tpu as pltpu
from jax.sharding import PartitionSpec as P

EPS = 1e-05
LANES = 256


def exchange(value, axis, bit):
    size = lax.axis_size(axis)
    return lax.ppermute(value, axis, [(i, i ^ bit) for i in range(size)])


def product_kernel(shard_ref, x_ref, gate_ref, up_ref, gate_mask_ref, up_mask_ref, own_ref, send_ref):
    rows = x_ref.shape[0] // 2
    for i, (weight_ref, mask_ref) in enumerate(((gate_ref, gate_mask_ref), (up_ref, up_mask_ref))):
        blocks = mask_ref.shape[0]
        side = weight_ref.shape[0] // blocks
        kept = jnp.concatenate(
            [
                weight_ref[b * side : (b + 1) * side, :] * mask_ref[b : b + 1, :].astype(jnp.bfloat16)
                for b in range(blocks)
            ],
            axis=0,
        )
        sums = jnp.dot(x_ref[...], kept, preferred_element_type=jnp.float32)
        own_ref[0, i] = sums[:rows]
        send_ref[0, i] = sums[rows:].astype(jnp.bfloat16)


def products(shard, x, gate_weight, up_weight, gate_mask, up_mask, piece, shards):
    depth, width = gate_weight.shape
    rows = x.shape[0] // 2
    per_shard = width // shards // LANES

    def column(p, shard_ref):
        other = 2 * lax.rem(p, shards // 2) + p // (shards // 2)
        return (0, (shard_ref[0] ^ other) * per_shard + piece)

    grid_spec = pltpu.PrefetchScalarGridSpec(
        num_scalar_prefetch=1,
        grid=(shards,),
        in_specs=[
            pl.BlockSpec(x.shape, lambda p, s: (0, 0)),
            pl.BlockSpec((depth, LANES), column),
            pl.BlockSpec((depth, LANES), column),
            pl.BlockSpec((gate_mask.shape[0], LANES), column),
            pl.BlockSpec((up_mask.shape[0], LANES), column),
        ],
        out_specs=[
            pl.BlockSpec((1, 2, rows, LANES), lambda p, s: (p, 0, 0, 0)),
            pl.BlockSpec((1, 2, rows, LANES), lambda p, s: (p, 0, 0, 0)),
        ],
    )
    return pl.pallas_call(
        product_kernel,
        grid_spec=grid_spec,
        out_shape=[
            jax.ShapeDtypeStruct((shards, 2, rows, LANES), jnp.float32),
            jax.ShapeDtypeStruct((shards, 2, rows, LANES), jnp.bfloat16),
        ],
        compiler_params=pltpu.CompilerParams(vmem_limit_bytes=32 * 1024 * 1024),
        cost_estimate=pl.CostEstimate(
            flops=2 * 2 * x.shape[0] * depth * LANES * shards,
            bytes_accessed=2 * depth * LANES * shards * 2 + 2 * shards * rows * LANES * 6,
            transcendentals=0,
        ),
        name="products",
    )(shard.reshape(1), x, gate_weight, up_weight, gate_mask, up_mask)


def local(tokens, gain, gate_weight, up_weight, gate_mask, up_mask):
    shards = lax.axis_size("tensor")
    shard = lax.axis_index("tensor")
    half = lax.axis_index("wide")
    depth, width = gate_weight.shape
    features = gain.shape[0]
    rows = tokens.shape[0]

    first, second = [], []
    for w in range(2):
        for t in range(shards):
            source = w * (shards // 2) + t // 2
            first.append(((t % 2) * shards + source, w * shards + t))
            second.append(((1 - t % 2) * shards + source, w * shards + t))
    mine = lax.dynamic_slice_in_dim(tokens, half * depth, depth, 1)
    theirs = lax.dynamic_slice_in_dim(tokens, (1 - half) * depth, depth, 1)
    a = lax.ppermute(mine, ("wide", "tensor"), first)
    b = lax.ppermute(theirs, ("wide", "tensor"), second)

    values = tokens.astype(jnp.float32)
    squares = jnp.sum(values * values, axis=-1).reshape(1, rows)
    bit = 1
    while bit < shards:
        squares = squares + exchange(squares, "tensor", bit)
        bit *= 2
    scale = lax.rsqrt(squares / features + EPS)
    scale_other = exchange(scale, "wide", 1)

    straight = (shard % 2) == half
    own_raw = jnp.where(straight, a, b)
    other_raw = jnp.where(straight, b, a)
    raw = jnp.concatenate([own_raw, other_raw], axis=0).astype(jnp.float32)
    scales = jnp.concatenate([scale, scale_other], axis=1).reshape(2 * rows, 1)
    first_row = half * (features // 2) + shard * depth
    gains = lax.dynamic_slice_in_dim(gain, first_row, depth, 0)
    normed = (raw * scales * gains[None, :]).astype(jnp.bfloat16)

    side = features // gate_mask.shape[0]
    first_block = first_row // side
    masks = []
    for mask in (gate_mask, up_mask):
        part = lax.dynamic_slice_in_dim(mask, first_block, depth // side, 0).astype(jnp.float32)
        masks.append(jnp.repeat(part, width // mask.shape[1], axis=1))

    outs = []
    for piece in range(width // shards // LANES):
        own, send = products(shard, normed, gate_weight, up_weight, *masks, piece, shards)
        from_core = exchange(send, "wide", 1)
        pairs = shards // 2
        to_pair = (own[pairs:] + from_core[pairs:].astype(jnp.float32)).astype(jnp.bfloat16)
        from_pair = exchange(to_pair, "tensor", 1)
        received = []
        for p in range(1, pairs):
            to_far = (
                own[p] + from_core[p].astype(jnp.float32) + from_pair[p].astype(jnp.float32)
            ).astype(jnp.bfloat16)
            received.append(exchange(to_far, "tensor", 2 * p))
        total = own[0] + from_core[0].astype(jnp.float32) + from_pair[0].astype(jnp.float32)
        for value in received:
            total = total + value.astype(jnp.float32)
        outs.append((jax.nn.silu(total[0]) * total[1]).astype(jnp.bfloat16))
    return jnp.concatenate(outs, axis=1)


def solution(mesh):
    in_specs = (
        P(("group", "wide"), "tensor"),
        P("group"),
        P(("group", "wide", "tensor"), None),
        P(("group", "wide", "tensor"), None),
        P("group", None),
        P("group", None),
    )
    out_specs = P(("group", "wide"), "tensor")
    return jax.shard_map(local, mesh=mesh, in_specs=in_specs, out_specs=out_specs, check_vma=False)
```

```python
import functools

import jax
import jax.numpy as jnp
from jax import lax
from jax.experimental import pallas as pl
from jax.experimental.pallas import tpu as pltpu
from jax.sharding import PartitionSpec as P

EPS = 1e-05
LANES = 128
VMEM_LIMIT = 52 * 1024 * 1024


def exchange(value, axis, bit):
    size = lax.axis_size(axis)
    return lax.ppermute(value, axis, [(i, i ^ bit) for i in range(size)])


def after(value, *earlier):
    return lax.optimization_barrier((value, *earlier))[0]


def cut_kernel(places, lanes, at_ref, gate_ref, up_ref, out_ref, held, in_sems, out_sems):
    weights = (gate_ref, up_ref)

    def copy_in(n, i):
        offset, start = places[n]
        first = pl.multiple_of((at_ref[0] ^ offset) * at_ref[2] + at_ref[1] + start, LANES)
        return pltpu.make_async_copy(weights[i].at[:, pl.ds(first, lanes)], held.at[n, i], in_sems.at[n, i])

    def copy_out(n, i):
        return pltpu.make_async_copy(held.at[n, i], out_ref.at[n, i], out_sems.at[n, i])

    every = [(n, i) for n in range(len(places)) for i in range(2)]
    for n, i in every:
        copy_in(n, i).start()
    for n, i in every:
        copy_in(n, i).wait()
        copy_out(n, i).start()
    for n, i in every:
        copy_out(n, i).wait()


def cut(at, gate_weight, up_weight, places, lanes):
    depth = gate_weight.shape[0]
    count = len(places)
    hbm = pl.BlockSpec(memory_space=pltpu.HBM)
    return pl.pallas_call(
        functools.partial(cut_kernel, places, lanes),
        in_specs=[pl.BlockSpec(memory_space=pltpu.SMEM), hbm, hbm],
        out_specs=hbm,
        out_shape=jax.ShapeDtypeStruct((count, 2, depth, lanes), jnp.bfloat16),
        scratch_shapes=[
            pltpu.VMEM((count, 2, depth, lanes), jnp.bfloat16),
            pltpu.SemaphoreType.DMA((count, 2)),
            pltpu.SemaphoreType.DMA((count, 2)),
        ],
        compiler_params=pltpu.CompilerParams(vmem_limit_bytes=VMEM_LIMIT),
        name="cut",
    )(at, gate_weight, up_weight)


def sums_kernel(places, lanes, side, stacked, at_ref, x_ref, gate_ref, up_ref, theirs_ref, masks_ref, *refs):
    out_refs, (kept, result, in_sems, out_sems) = refs[:-4], refs[-4:]
    depth = gate_ref.shape[0]
    weights = (gate_ref, up_ref)
    firsts = [
        pl.multiple_of((at_ref[0] ^ offset) * at_ref[2] + at_ref[1] + start, LANES) for offset, start, _ in places
    ]

    def copies_in(n, i):
        return (
            pltpu.make_async_copy(
                weights[i].at[:, pl.ds(firsts[n], lanes)], kept.at[n, i, pl.ds(0, depth)], in_sems.at[n, i, 0]
            ),
            pltpu.make_async_copy(
                theirs_ref.at[places[n][2], i], kept.at[n, i, pl.ds(depth, depth)], in_sems.at[n, i, 1]
            ),
        )

    def copy_out(n, i):
        out = out_refs[0].at[n, i] if stacked else out_refs[n].at[i]
        return pltpu.make_async_copy(result.at[n, i], out, out_sems.at[n, i])

    every = [(n, i) for n in range(len(places)) for i in range(2)]
    ahead = 3
    for one in every[:ahead]:
        for copy in copies_in(*one):
            copy.start()
    across = masks_ref.shape[1]
    blocks = 2 * depth // side
    for k, (n, i) in enumerate(every):
        if k + ahead < len(every):
            for copy in copies_in(*every[k + ahead]):
                copy.start()
        if i == 0:
            block = lax.broadcasted_iota(jnp.int32, (across, lanes), 0)
            column = firsts[n] + lax.broadcasted_iota(jnp.int32, (across, lanes), 1)
            spread = ((column >= block * side) & (column < (block + 1) * side)).astype(jnp.bfloat16)
            masks = jnp.dot(masks_ref[...], spread, preferred_element_type=jnp.float32).astype(jnp.bfloat16)
        for copy in copies_in(n, i):
            copy.wait()
        for b in range(blocks):
            rows = slice(b * side, (b + 1) * side)
            kept[n, i, rows, :] = kept[n, i, rows, :] * masks[i * blocks + b : i * blocks + b + 1, :]
        total = jnp.dot(x_ref[...], kept[n, i], preferred_element_type=jnp.float32)
        result[n, i] = total.astype(result.dtype)
        copy_out(n, i).start()
    for one in every:
        copy_out(*one).wait()


def sums(at, x, gate_weight, up_weight, theirs, masks, side, places, lanes, dtype, stacked):
    depth = gate_weight.shape[0]
    tokens = x.shape[0]
    count = len(places)
    vmem = pl.BlockSpec(memory_space=pltpu.VMEM)
    hbm = pl.BlockSpec(memory_space=pltpu.HBM)
    return pl.pallas_call(
        functools.partial(sums_kernel, places, lanes, side, stacked),
        in_specs=[pl.BlockSpec(memory_space=pltpu.SMEM), vmem, hbm, hbm, hbm, vmem],
        out_specs=[hbm] * (1 if stacked else count),
        out_shape=(
            [jax.ShapeDtypeStruct((count, 2, tokens, lanes), dtype)]
            if stacked
            else [jax.ShapeDtypeStruct((2, tokens, lanes), dtype)] * count
        ),
        scratch_shapes=[
            pltpu.VMEM((count, 2, 2 * depth, lanes), jnp.bfloat16),
            pltpu.VMEM((count, 2, tokens, lanes), dtype),
            pltpu.SemaphoreType.DMA((count, 2, 2)),
            pltpu.SemaphoreType.DMA((count, 2)),
        ],
        compiler_params=pltpu.CompilerParams(vmem_limit_bytes=VMEM_LIMIT),
        name="sums",
    )(at, x, gate_weight, up_weight, theirs, masks)


def local(tokens, gain, gate_weight, up_weight, gate_mask, up_mask):
    shards = lax.axis_size("tensor")
    shard = lax.axis_index("tensor")
    half = lax.axis_index("wide")
    depth, width = gate_weight.shape
    features = gain.shape[0]
    rows = tokens.shape[0]
    per_shard = width // shards
    per_core = per_shard // 2
    pairs = shards // 2

    mine = jnp.stack([shard, half * per_core, per_shard]).astype(jnp.int32)
    partners = jnp.stack([shard, (1 - half) * per_core, per_shard]).astype(jnp.int32)
    side = features // gate_mask.shape[0]
    first_rows = [half * (features // 2) + shard * depth, (1 - half) * (features // 2) + shard * depth]
    lanes = per_core // 2 if pairs == 4 else per_core
    theirs, pair, far = {}, {}, {}

    def place(unit):
        p, y, h = unit
        return (2 * p + y, h * lanes)

    latest = []

    def in_turn(value, *more):
        return after(value, *latest, *more)

    def emit(value):
        latest[:] = [value]
        return value

    def fetch(units, *earlier):
        value = emit(cut(in_turn(partners, *earlier), gate_weight, up_weight, tuple(map(place, units)), lanes))
        value = exchange(value, "wide", 1)
        for n, unit in enumerate(units):
            theirs[unit] = (value, n)

    raw = []
    for flip in range(2):
        moves = []
        for w in range(2):
            for t in range(shards):
                moves.append((((t % 2) ^ flip) * shards + w * pairs + t // 2, w * shards + t))
        piece = lax.dynamic_slice_in_dim(tokens, (half ^ flip) * depth, depth, 1)
        raw.append(lax.ppermute(piece, ("wide", "tensor"), moves))
    values = tokens.astype(jnp.float32)
    squares = jnp.sum(values * values, axis=-1).reshape(1, rows)
    emit(squares)
    if pairs == 4:
        fetch([(3, 1, 0), (3, 1, 1)])
    total = squares + exchange(squares, "tensor", 2)
    if pairs == 4:
        emit(total)
        fetch([(3, 0, 0), (3, 0, 1), (2, 1, 0), (1, 1, 0)])
    raw = after(jnp.where(shard % 2 == 1, jnp.concatenate(raw[::-1]), jnp.concatenate(raw)), total)
    raw_other = exchange(raw, "wide", 1)
    bit = 4
    while bit < shards:
        total = total + exchange(total, "tensor", bit)
        bit *= 2
    if pairs == 4:
        emit(total)
        fetch([(2, 1, 1), (1, 1, 1), (2, 0, 0), (1, 0, 0), (0, 0, 0), (0, 0, 1)])
    total = total + exchange(total, "tensor", 1)
    scale = lax.rsqrt(total / features + EPS)
    scale_other = exchange(scale, "wide", 1)
    scales = jnp.where(
        half == 0,
        jnp.concatenate([scale, scale_other], axis=1),
        jnp.concatenate([scale_other, scale], axis=1),
    ).reshape(2 * rows, 1)
    gains = [lax.dynamic_slice_in_dim(gain, r, depth, 0)[None, :] for r in first_rows]
    normed = jnp.concatenate(
        [(v.astype(jnp.float32) * scales * g).astype(jnp.bfloat16) for v, g in zip((raw, raw_other), gains)], axis=1
    )

    masks = jnp.concatenate(
        [
            lax.dynamic_slice_in_dim(mask, r // side, depth // side, 0)
            for mask in (gate_mask, up_mask)
            for r in first_rows
        ]
    ).astype(jnp.bfloat16)

    def chip_sums(units, *more, stacked=True):
        value = theirs[units[0]][0]
        places = tuple((*place(unit), theirs[unit][1]) for unit in units)
        dtype = jnp.bfloat16 if stacked else jnp.float32
        values = sums(
            mine, in_turn(normed, *more), gate_weight, up_weight, value, masks, side, places, lanes, dtype, stacked
        )
        emit(values[0])
        return values[0] if stacked else values

    def finish(own, *terms):
        total = in_turn(own)
        for term in terms:
            total = total + wide(term)
        return (jax.nn.silu(total[0]) * total[1]).astype(jnp.bfloat16)

    def add(own, *terms):
        total = in_turn(own)
        for term in terms:
            total = total + wide(term)
        return emit(total.astype(jnp.bfloat16))

    def give(hidden):
        keep = lax.dynamic_slice_in_dim(hidden, half * rows, rows, 0)
        got = exchange(lax.dynamic_slice_in_dim(hidden, (1 - half) * rows, rows, 0), "wide", 1)
        return jnp.where(half == 0, keep, got), jnp.where(half == 0, got, keep)

    wide = lambda value: value.astype(jnp.float32)

    if pairs == 4:
        tensor_pairs = lambda moves: [(2 * i + y, 2 * j + y) for i, j in moves for y in range(2)]
        by_neighbour = tensor_pairs(((0, 1), (3, 2)))
        middle = tensor_pairs(((1, 2), (2, 1)))

        pair3 = exchange(chip_sums([(3, 1, 0), (3, 1, 1)]), "tensor", 1)
        fetch([(2, 0, 1), (1, 0, 1)])
        fetch([(0, 1, 0), (0, 1, 1)])
        near3 = chip_sums([(3, 0, 0), (3, 0, 1)], stacked=False)
        far_a = chip_sums([(2, 1, 0), (1, 1, 0)])
        pair_a = exchange(in_turn(far_a, pair3), "tensor", 1)
        third = jnp.stack([add(near3[h], pair3[h]) for h in range(2)])
        relay = lax.ppermute(third, "tensor", by_neighbour)
        across = lax.ppermute(third, "tensor", middle)
        near_a = chip_sums([(2, 0, 0), (1, 0, 0)], stacked=False)
        far_b = chip_sums([(2, 1, 1), (1, 1, 1)])
        pair_b = exchange(in_turn(far_b, pair_a), "tensor", 1)
        second_a = exchange(add(after(near_a[0], across), pair_a[0], relay[0]), "tensor", 4)
        first_a = exchange(add(near_a[1], pair_a[1]), "tensor", 2)
        near_b = chip_sums([(2, 0, 1), (1, 0, 1)], stacked=False)
        far_0 = chip_sums([(0, 1, 0), (0, 1, 1)])
        pair_0 = exchange(in_turn(far_0, pair_b), "tensor", 1)
        second_b = exchange(add(near_b[0], pair_b[0], relay[1]), "tensor", 4)
        first_b = exchange(add(near_b[1], pair_b[1]), "tensor", 2)
        own = chip_sums([(0, 0, 0), (0, 0, 1)], stacked=False)
        left, right = [], []
        for h, second, first in ((0, second_a, first_a), (1, second_b, first_b)):
            one, other = give(finish(own[h], pair_0[h], first, second, across[h]))
            left.append(one)
            right.append(other)
        return jnp.concatenate(left + right, axis=1)
    received = []
    for p in range(pairs - 1, -1, -1):
        fetch([(p, 1, 0), (p, 0, 0)])
        from_pair = exchange(chip_sums([(p, 1, 0)])[0], "tensor", 1)
        own = chip_sums([(p, 0, 0)], stacked=False)[0]
        if p:
            received.append(exchange(add(own, from_pair), "tensor", 2 * p))
    return jnp.concatenate(give(finish(own, from_pair, *received)), axis=1)


def solution(mesh):
    in_specs = (
        P(("group", "wide"), "tensor"),
        P("group"),
        P(("group", "wide", "tensor"), None),
        P(("group", "wide", "tensor"), None),
        P("group", None),
        P("group", None),
    )
    out_specs = P(("group", "wide"), "tensor")
    return jax.shard_map(local, mesh=mesh, in_specs=in_specs, out_specs=out_specs, check_vma=False)
```

```python
import functools

import jax
import jax.numpy as jnp
from jax import lax
from jax.experimental import pallas as pl
from jax.experimental.pallas import tpu as pltpu
from jax.sharding import PartitionSpec as P

EPS = 1e-05
LANES = 128
VMEM_LIMIT = 52 * 1024 * 1024


def exchange(value, axis, bit):
    size = lax.axis_size(axis)
    return lax.ppermute(value, axis, [(i, i ^ bit) for i in range(size)])


def after(value, *earlier):
    return lax.optimization_barrier((value, *earlier))[0]


def cut_kernel(groups, lanes, at_ref, gate_ref, up_ref, *refs):
    out_refs, (held, in_sems, out_sems) = refs[:-3], refs[-3:]
    weights = (gate_ref, up_ref)
    every = []
    for places, out_ref in zip(groups, out_refs):
        for n, (offset, start) in enumerate(places):
            first = pl.multiple_of((at_ref[0] ^ offset) * at_ref[2] + at_ref[1] + start, LANES)
            for i in range(2):
                k = len(every)
                every.append(
                    (
                        pltpu.make_async_copy(weights[i].at[:, pl.ds(first, lanes)], held.at[k], in_sems.at[k]),
                        pltpu.make_async_copy(held.at[k], out_ref.at[n, i], out_sems.at[k]),
                    )
                )
    ahead = 6
    for copy_in, _ in every[:ahead]:
        copy_in.start()
    for k, (copy_in, copy_out) in enumerate(every):
        copy_in.wait()
        copy_out.start()
        if k + ahead < len(every):
            every[k + ahead][0].start()
    for _, copy_out in every:
        copy_out.wait()


def cut(at, gate_weight, up_weight, groups, lanes):
    depth = gate_weight.shape[0]
    count = 2 * sum(map(len, groups))
    hbm = pl.BlockSpec(memory_space=pltpu.HBM)
    return pl.pallas_call(
        functools.partial(cut_kernel, groups, lanes),
        in_specs=[pl.BlockSpec(memory_space=pltpu.SMEM), hbm, hbm],
        out_specs=[hbm] * len(groups),
        out_shape=[jax.ShapeDtypeStruct((len(places), 2, depth, lanes), jnp.bfloat16) for places in groups],
        scratch_shapes=[
            pltpu.VMEM((count, depth, lanes), jnp.bfloat16),
            pltpu.SemaphoreType.DMA((count,)),
            pltpu.SemaphoreType.DMA((count,)),
        ],
        compiler_params=pltpu.CompilerParams(vmem_limit_bytes=VMEM_LIMIT),
        name="cut",
    )(at, gate_weight, up_weight)


def sums_kernel(places, lanes, side, stacked, at_ref, x_ref, gate_ref, up_ref, theirs_ref, masks_ref, *refs):
    out_refs, (kept, result, in_sems, out_sems) = refs[:-4], refs[-4:]
    depth = gate_ref.shape[0]
    weights = (gate_ref, up_ref)
    firsts = [
        pl.multiple_of((at_ref[0] ^ offset) * at_ref[2] + at_ref[1] + start, LANES) for offset, start, _ in places
    ]

    def copies_in(n, i):
        return (
            pltpu.make_async_copy(
                weights[i].at[:, pl.ds(firsts[n], lanes)], kept.at[n, i, pl.ds(0, depth)], in_sems.at[n, i, 0]
            ),
            pltpu.make_async_copy(
                theirs_ref.at[places[n][2], i], kept.at[n, i, pl.ds(depth, depth)], in_sems.at[n, i, 1]
            ),
        )

    def copy_out(n, i):
        out = out_refs[0].at[n, i] if stacked else out_refs[n].at[i]
        return pltpu.make_async_copy(result.at[n, i], out, out_sems.at[n, i])

    every = [(n, i) for n in range(len(places)) for i in range(2)]
    ahead = 3
    for one in every[:ahead]:
        for copy in copies_in(*one):
            copy.start()
    across = masks_ref.shape[1]
    blocks = 2 * depth // side
    for k, (n, i) in enumerate(every):
        if k + ahead < len(every):
            for copy in copies_in(*every[k + ahead]):
                copy.start()
        if i == 0:
            block = lax.broadcasted_iota(jnp.int32, (across, lanes), 0)
            column = firsts[n] + lax.broadcasted_iota(jnp.int32, (across, lanes), 1)
            spread = ((column >= block * side) & (column < (block + 1) * side)).astype(jnp.bfloat16)
            masks = jnp.dot(masks_ref[...], spread, preferred_element_type=jnp.float32).astype(jnp.bfloat16)
        for copy in copies_in(n, i):
            copy.wait()
        for b in range(blocks):
            rows = slice(b * side, (b + 1) * side)
            kept[n, i, rows, :] = kept[n, i, rows, :] * masks[i * blocks + b : i * blocks + b + 1, :]
        total = jnp.dot(x_ref[...], kept[n, i], preferred_element_type=jnp.float32)
        result[n, i] = total.astype(result.dtype)
        copy_out(n, i).start()
    for one in every:
        copy_out(*one).wait()


def sums(at, x, gate_weight, up_weight, theirs, masks, side, places, lanes, dtype, stacked):
    depth = gate_weight.shape[0]
    tokens = x.shape[0]
    count = len(places)
    vmem = pl.BlockSpec(memory_space=pltpu.VMEM)
    hbm = pl.BlockSpec(memory_space=pltpu.HBM)
    return pl.pallas_call(
        functools.partial(sums_kernel, places, lanes, side, stacked),
        in_specs=[pl.BlockSpec(memory_space=pltpu.SMEM), vmem, hbm, hbm, hbm, vmem],
        out_specs=[hbm] * (1 if stacked else count),
        out_shape=(
            [jax.ShapeDtypeStruct((count, 2, tokens, lanes), dtype)]
            if stacked
            else [jax.ShapeDtypeStruct((2, tokens, lanes), dtype)] * count
        ),
        scratch_shapes=[
            pltpu.VMEM((count, 2, 2 * depth, lanes), jnp.bfloat16),
            pltpu.VMEM((count, 2, tokens, lanes), dtype),
            pltpu.SemaphoreType.DMA((count, 2, 2)),
            pltpu.SemaphoreType.DMA((count, 2)),
        ],
        compiler_params=pltpu.CompilerParams(vmem_limit_bytes=VMEM_LIMIT),
        name="sums",
    )(at, x, gate_weight, up_weight, theirs, masks)


def local(tokens, gain, gate_weight, up_weight, gate_mask, up_mask):
    shards = lax.axis_size("tensor")
    shard = lax.axis_index("tensor")
    half = lax.axis_index("wide")
    depth, width = gate_weight.shape
    features = gain.shape[0]
    rows = tokens.shape[0]
    per_shard = width // shards
    per_core = per_shard // 2
    pairs = shards // 2

    mine = jnp.stack([shard, half * per_core, per_shard]).astype(jnp.int32)
    partners = jnp.stack([shard, (1 - half) * per_core, per_shard]).astype(jnp.int32)
    side = features // gate_mask.shape[0]
    first_rows = [half * (features // 2) + shard * depth, (1 - half) * (features // 2) + shard * depth]
    lanes = per_core // 2 if pairs == 4 else per_core
    theirs, pair, far = {}, {}, {}

    def place(unit):
        p, y, h = unit
        return (2 * p + y, h * lanes)

    latest = []

    def in_turn(value, *more):
        return after(value, *latest, *more)

    def emit(value):
        latest[:] = [value]
        return value

    def fetch(*groups):
        values = cut(
            in_turn(partners), gate_weight, up_weight, tuple(tuple(map(place, units)) for units in groups), lanes
        )
        emit(values[0])
        for units, value in zip(groups, values):
            value = exchange(value, "wide", 1)
            for n, unit in enumerate(units):
                theirs[unit] = (value, n)

    raw = []
    for flip in range(2):
        moves = []
        for w in range(2):
            for t in range(shards):
                moves.append((((t % 2) ^ flip) * shards + w * pairs + t // 2, w * shards + t))
        piece = lax.dynamic_slice_in_dim(tokens, (half ^ flip) * depth, depth, 1)
        raw.append(lax.ppermute(piece, ("wide", "tensor"), moves))
    values = tokens.astype(jnp.float32)
    squares = jnp.sum(values * values, axis=-1).reshape(1, rows)
    emit(squares)
    if pairs == 4:
        fetch([(3, 1, 0), (3, 1, 1)])
    total = squares
    for p in range(1, pairs):
        total = total + exchange(squares, "tensor", 2 * p)
    raw = jnp.where(shard % 2 == 1, jnp.concatenate(raw[::-1]), jnp.concatenate(raw))
    raw_other = exchange(after(raw, total), "wide", 1)
    total = total + exchange(after(total, raw), "tensor", 1)
    scale = lax.rsqrt(total / features + EPS)
    scale_other = exchange(scale, "wide", 1)
    scales = jnp.where(
        half == 0,
        jnp.concatenate([scale, scale_other], axis=1),
        jnp.concatenate([scale_other, scale], axis=1),
    ).reshape(2 * rows, 1)
    gains = [lax.dynamic_slice_in_dim(gain, r, depth, 0)[None, :] for r in first_rows]
    normed = jnp.concatenate(
        [(v.astype(jnp.float32) * scales * g).astype(jnp.bfloat16) for v, g in zip((raw, raw_other), gains)], axis=1
    )

    emit(normed)
    if pairs == 4:
        latest.append(theirs[3, 1, 0][0])
        fetch(
            [(3, 0, 0), (3, 0, 1), (2, 1, 0), (1, 1, 0)],
            [(2, 1, 1), (1, 1, 1), (2, 0, 0), (1, 0, 0), (0, 0, 0), (0, 0, 1)],
        )

    masks = jnp.concatenate(
        [
            lax.dynamic_slice_in_dim(mask, r // side, depth // side, 0)
            for mask in (gate_mask, up_mask)
            for r in first_rows
        ]
    ).astype(jnp.bfloat16)

    def chip_sums(units, *more, stacked=True):
        value = theirs[units[0]][0]
        places = tuple((*place(unit), theirs[unit][1]) for unit in units)
        dtype = jnp.bfloat16 if stacked else jnp.float32
        values = sums(
            mine, in_turn(normed, *more), gate_weight, up_weight, value, masks, side, places, lanes, dtype, stacked
        )
        emit(values[0])
        return values[0] if stacked else values

    def finish(own, *terms):
        total = in_turn(own)
        for term in terms:
            total = total + wide(term)
        return (jax.nn.silu(total[0]) * total[1]).astype(jnp.bfloat16)

    def add(own, *terms):
        total = in_turn(own)
        for term in terms:
            total = total + wide(term)
        return emit(total.astype(jnp.bfloat16))

    def give(hidden):
        keep = lax.dynamic_slice_in_dim(hidden, half * rows, rows, 0)
        got = exchange(lax.dynamic_slice_in_dim(hidden, (1 - half) * rows, rows, 0), "wide", 1)
        return jnp.where(half == 0, keep, got), jnp.where(half == 0, got, keep)

    wide = lambda value: value.astype(jnp.float32)

    if pairs == 4:
        tensor_pairs = lambda moves: [(2 * i + y, 2 * j + y) for i, j in moves for y in range(2)]
        by_neighbour = tensor_pairs(((0, 1), (3, 2)))
        middle = tensor_pairs(((1, 2), (2, 1)))

        pair3 = exchange(chip_sums([(3, 1, 0), (3, 1, 1)]), "tensor", 1)
        fetch([(2, 0, 1), (1, 0, 1)], [(0, 1, 0), (0, 1, 1)])
        near3 = chip_sums([(3, 0, 0), (3, 0, 1)], stacked=False)
        far_a = chip_sums([(2, 1, 0), (1, 1, 0)])
        pair_a = exchange(in_turn(far_a, pair3), "tensor", 1)
        third = jnp.stack([add(near3[h], pair3[h]) for h in range(2)])
        relay = lax.ppermute(third, "tensor", by_neighbour)
        across = lax.ppermute(third, "tensor", middle)
        near_a = chip_sums([(2, 0, 0), (1, 0, 0)], stacked=False)
        far_b = chip_sums([(2, 1, 1), (1, 1, 1)])
        pair_b = exchange(in_turn(far_b, pair_a), "tensor", 1)
        second_a = exchange(add(after(near_a[0], across), pair_a[0], relay[0]), "tensor", 4)
        first_a = exchange(add(near_a[1], pair_a[1]), "tensor", 2)
        near_b = chip_sums([(2, 0, 1), (1, 0, 1)], stacked=False)
        far_0 = chip_sums([(0, 1, 0), (0, 1, 1)])
        pair_0 = exchange(in_turn(far_0, pair_b), "tensor", 1)
        second_b = exchange(add(near_b[0], pair_b[0], relay[1]), "tensor", 4)
        first_b = exchange(add(near_b[1], pair_b[1]), "tensor", 2)
        own = chip_sums([(0, 0, 0), (0, 0, 1)], stacked=False)
        one, other = give(finish(own[0], pair_0[0], first_a, second_a, across[0]))
        two, another = give(finish(own[1], pair_0[1], first_b, second_b, across[1]))
        return jnp.concatenate([one, two, other, another], axis=1)
    received = []
    for p in range(pairs - 1, -1, -1):
        fetch([(p, 1, 0), (p, 0, 0)])
        from_pair = exchange(chip_sums([(p, 1, 0)])[0], "tensor", 1)
        own = chip_sums([(p, 0, 0)], stacked=False)[0]
        if p:
            received.append(exchange(add(own, from_pair), "tensor", 2 * p))
    return jnp.concatenate(give(finish(own, from_pair, *received)), axis=1)


def solution(mesh):
    in_specs = (
        P(("group", "wide"), "tensor"),
        P("group"),
        P(("group", "wide", "tensor"), None),
        P(("group", "wide", "tensor"), None),
        P("group", None),
        P("group", None),
    )
    out_specs = P(("group", "wide"), "tensor")
    return jax.shard_map(local, mesh=mesh, in_specs=in_specs, out_specs=out_specs, check_vma=False)
```

```python
import functools

import jax
import jax.numpy as jnp
from jax import lax
from jax.experimental import pallas as pl
from jax.experimental.pallas import tpu as pltpu
from jax.sharding import PartitionSpec as P

EPS = 1e-05
LANES = 128
VMEM_LIMIT = 52 * 1024 * 1024


def exchange(value, axis, bit):
    size = lax.axis_size(axis)
    return lax.ppermute(value, axis, [(i, i ^ bit) for i in range(size)])


def after(value, *earlier):
    return lax.optimization_barrier((value, *earlier))[0]


def cut_copies(groups, lanes, at_ref, gate_ref, up_ref, out_refs, held, in_sems, out_sems):
    weights = (gate_ref, up_ref)
    every = []
    for places, out_ref in zip(groups, out_refs):
        for n, (offset, start) in enumerate(places):
            first = pl.multiple_of((at_ref[0] ^ offset) * at_ref[2] + at_ref[1] + start, LANES)
            for i in range(2):
                k = len(every)
                every.append(
                    (
                        pltpu.make_async_copy(weights[i].at[:, pl.ds(first, lanes)], held.at[k], in_sems.at[k]),
                        pltpu.make_async_copy(held.at[k], out_ref.at[n, i], out_sems.at[k]),
                    )
                )
    return every


def cut_scratch(groups, depth, lanes):
    count = 2 * sum(map(len, groups))
    return [
        pltpu.VMEM((count, depth, lanes), jnp.bfloat16),
        pltpu.SemaphoreType.DMA((count,)),
        pltpu.SemaphoreType.DMA((count,)),
    ]


def cut_kernel(groups, lanes, at_ref, gate_ref, up_ref, *refs):
    every = cut_copies(groups, lanes, at_ref, gate_ref, up_ref, refs[:-3], *refs[-3:])
    for copy_in, _ in every:
        copy_in.start()
    for copy_in, copy_out in every:
        copy_in.wait()
        copy_out.start()
    for _, copy_out in every:
        copy_out.wait()


def cut(at, gate_weight, up_weight, groups, lanes):
    depth = gate_weight.shape[0]
    hbm = pl.BlockSpec(memory_space=pltpu.HBM)
    return pl.pallas_call(
        functools.partial(cut_kernel, groups, lanes),
        in_specs=[pl.BlockSpec(memory_space=pltpu.SMEM), hbm, hbm],
        out_specs=[hbm] * len(groups),
        out_shape=[jax.ShapeDtypeStruct((len(places), 2, depth, lanes), jnp.bfloat16) for places in groups],
        scratch_shapes=cut_scratch(groups, depth, lanes),
        compiler_params=pltpu.CompilerParams(vmem_limit_bytes=VMEM_LIMIT),
        name="cut",
    )(at, gate_weight, up_weight)


def sums_kernel(
    places, lanes, side, stacked, groups, messages, at_ref, partner_ref, x_ref, gate_ref, up_ref, masks_ref, *refs
):
    theirs_refs, refs = refs[:messages], refs[messages:]
    outs = 1 if stacked else len(places)
    out_refs, refs = refs[:outs], refs[outs:]
    cut_refs, refs = refs[: len(groups)], refs[len(groups) :]
    kept, result, in_sems, out_sems = refs[:4]
    depth = gate_ref.shape[0]
    weights = (gate_ref, up_ref)
    firsts = [
        pl.multiple_of((at_ref[0] ^ offset) * at_ref[2] + at_ref[1] + start, LANES) for offset, start, *_ in places
    ]

    def copies_in(n, i):
        return (
            pltpu.make_async_copy(
                weights[i].at[:, pl.ds(firsts[n], lanes)], kept.at[n, i, pl.ds(0, depth)], in_sems.at[n, i, 0]
            ),
            pltpu.make_async_copy(
                theirs_refs[places[n][2]].at[places[n][3], i], kept.at[n, i, pl.ds(depth, depth)], in_sems.at[n, i, 1]
            ),
        )

    def copy_out(n, i):
        out = out_refs[0].at[n, i] if stacked else out_refs[n].at[i]
        return pltpu.make_async_copy(result.at[n, i], out, out_sems.at[n, i])

    every = [(n, i) for n in range(len(places)) for i in range(2)]
    ahead = 3
    for one in every[:ahead]:
        for copy in copies_in(*one):
            copy.start()
    cuts = cut_copies(groups, lanes, partner_ref, gate_ref, up_ref, cut_refs, *refs[4:]) if groups else []
    for copy_in, _ in cuts:
        copy_in.start()
    across = masks_ref.shape[1]
    blocks = 2 * depth // side
    for k, (n, i) in enumerate(every):
        if k + ahead < len(every):
            for copy in copies_in(*every[k + ahead]):
                copy.start()
        if i == 0:
            block = lax.broadcasted_iota(jnp.int32, (across, lanes), 0)
            column = firsts[n] + lax.broadcasted_iota(jnp.int32, (across, lanes), 1)
            spread = ((column >= block * side) & (column < (block + 1) * side)).astype(jnp.bfloat16)
            masks = jnp.dot(masks_ref[...], spread, preferred_element_type=jnp.float32).astype(jnp.bfloat16)
        for copy in copies_in(n, i):
            copy.wait()
        for b in range(blocks):
            rows = slice(b * side, (b + 1) * side)
            kept[n, i, rows, :] = kept[n, i, rows, :] * masks[i * blocks + b : i * blocks + b + 1, :]
        total = jnp.dot(x_ref[...], kept[n, i], preferred_element_type=jnp.float32)
        result[n, i] = total.astype(result.dtype)
        copy_out(n, i).start()
    for copy_in, copy_out_cut in cuts:
        copy_in.wait()
        copy_out_cut.start()
    for one in every:
        copy_out(*one).wait()
    for _, copy_out_cut in cuts:
        copy_out_cut.wait()


def sums(at, x, gate_weight, up_weight, theirs, masks, side, places, lanes, dtype, stacked, partner, groups):
    depth = gate_weight.shape[0]
    tokens = x.shape[0]
    count = len(places)
    vmem = pl.BlockSpec(memory_space=pltpu.VMEM)
    hbm = pl.BlockSpec(memory_space=pltpu.HBM)
    return pl.pallas_call(
        functools.partial(sums_kernel, places, lanes, side, stacked, groups, len(theirs)),
        in_specs=[pl.BlockSpec(memory_space=pltpu.SMEM)] * 2 + [vmem, hbm, hbm, vmem] + [hbm] * len(theirs),
        out_specs=[hbm] * ((1 if stacked else count) + len(groups)),
        out_shape=(
            [jax.ShapeDtypeStruct((count, 2, tokens, lanes), dtype)]
            if stacked
            else [jax.ShapeDtypeStruct((2, tokens, lanes), dtype)] * count
        )
        + [jax.ShapeDtypeStruct((len(units), 2, depth, lanes), jnp.bfloat16) for units in groups],
        scratch_shapes=[
            pltpu.VMEM((count, 2, 2 * depth, lanes), jnp.bfloat16),
            pltpu.VMEM((count, 2, tokens, lanes), dtype),
            pltpu.SemaphoreType.DMA((count, 2, 2)),
            pltpu.SemaphoreType.DMA((count, 2)),
        ]
        + (cut_scratch(groups, depth, lanes) if groups else []),
        compiler_params=pltpu.CompilerParams(vmem_limit_bytes=VMEM_LIMIT),
        name="sums",
    )(at, partner, x, gate_weight, up_weight, masks, *theirs)


def local(tokens, gain, gate_weight, up_weight, gate_mask, up_mask):
    shards = lax.axis_size("tensor")
    shard = lax.axis_index("tensor")
    half = lax.axis_index("wide")
    depth, width = gate_weight.shape
    features = gain.shape[0]
    rows = tokens.shape[0]
    per_shard = width // shards
    per_core = per_shard // 2
    pairs = shards // 2

    mine = jnp.stack([shard, half * per_core, per_shard]).astype(jnp.int32)
    partners = jnp.stack([shard, (1 - half) * per_core, per_shard]).astype(jnp.int32)
    side = features // gate_mask.shape[0]
    first_rows = [half * (features // 2) + shard * depth, (1 - half) * (features // 2) + shard * depth]
    lanes = per_core // 2 if pairs == 4 else per_core
    theirs, pair, far = {}, {}, {}

    def place(unit):
        p, y, h = unit
        return (2 * p + y, h * lanes)

    latest = []

    def in_turn(value, *more):
        return after(value, *latest, *more)

    def emit(value):
        latest[:] = [value]
        return value

    def in_place(groups):
        return tuple(tuple(map(place, units)) for units in groups)

    def swap(groups, values):
        for units, value in zip(groups, values):
            value = exchange(value, "wide", 1)
            for n, unit in enumerate(units):
                theirs[unit] = (value, n)

    def fetch(*groups):
        values = cut(in_turn(partners), gate_weight, up_weight, in_place(groups), lanes)
        emit(values[0])
        swap(groups, values)

    raw = []
    for flip in range(2):
        moves = []
        for w in range(2):
            for t in range(shards):
                moves.append((((t % 2) ^ flip) * shards + w * pairs + t // 2, w * shards + t))
        piece = lax.dynamic_slice_in_dim(tokens, (half ^ flip) * depth, depth, 1)
        raw.append(lax.ppermute(piece, ("wide", "tensor"), moves))
    values = tokens.astype(jnp.float32)
    squares = jnp.sum(values * values, axis=-1).reshape(1, rows)
    total = squares
    for p in range(1, pairs):
        total = total + exchange(squares, "tensor", 2 * p)
    raw = jnp.where(shard % 2 == 1, jnp.concatenate(raw[::-1]), jnp.concatenate(raw))
    masks = jnp.concatenate(
        [
            lax.dynamic_slice_in_dim(mask, r // side, depth // side, 0)
            for mask in (gate_mask, up_mask)
            for r in first_rows
        ]
    ).astype(jnp.bfloat16)
    gains = jnp.stack([lax.dynamic_slice_in_dim(gain, r, depth, 0) for r in first_rows])
    latest[:] = [total, raw, masks, gains]
    if pairs == 4:
        fetch([(3, 1, 0), (3, 1, 1)])
    raw_other = exchange(after(raw, total), "wide", 1)
    total = total + exchange(after(total, raw), "tensor", 1)
    scale = lax.rsqrt(total / features + EPS)
    scale_other = exchange(scale, "wide", 1)
    scales = jnp.where(
        half == 0,
        jnp.concatenate([scale, scale_other], axis=1),
        jnp.concatenate([scale_other, scale], axis=1),
    ).reshape(2 * rows, 1)
    normed = jnp.concatenate(
        [(v.astype(jnp.float32) * scales * gains[i : i + 1]).astype(jnp.bfloat16) for i, v in enumerate((raw, raw_other))], axis=1
    )

    emit(normed)

    def chip_sums(units, stacked=True, groups=()):
        messages = []
        for unit in units:
            if not any(theirs[unit][0] is message for message in messages):
                messages.append(theirs[unit][0])
        places = tuple(
            (*place(unit), [theirs[unit][0] is m for m in messages].index(True), theirs[unit][1]) for unit in units
        )
        dtype = jnp.bfloat16 if stacked else jnp.float32
        values = sums(
            mine, in_turn(normed), gate_weight, up_weight, messages, masks, side, places, lanes, dtype, stacked,
            partners, in_place(groups)
        )
        emit(values[0])
        outs = 1 if stacked else len(units)
        swap(groups, values[outs:])
        return values[0] if stacked else values

    def finish(own, *terms):
        total = in_turn(own)
        for term in terms:
            total = total + wide(term)
        return (jax.nn.silu(total[0]) * total[1]).astype(jnp.bfloat16)

    def add(own, *terms):
        total = in_turn(own)
        for term in terms:
            total = total + wide(term)
        return emit(total.astype(jnp.bfloat16))

    def give(hidden):
        keep = lax.dynamic_slice_in_dim(hidden, half * rows, rows, 0)
        got = exchange(lax.dynamic_slice_in_dim(hidden, (1 - half) * rows, rows, 0), "wide", 1)
        return jnp.where(half == 0, keep, got), jnp.where(half == 0, got, keep)

    wide = lambda value: value.astype(jnp.float32)

    if pairs == 4:
        tensor_pairs = lambda moves: [(2 * i + y, 2 * j + y) for i, j in moves for y in range(2)]
        by_neighbour = tensor_pairs(((0, 1), (3, 2)))
        middle = tensor_pairs(((1, 2), (2, 1)))

        far_3 = chip_sums(
            [(3, 1, 0), (3, 1, 1)],
            groups=[
                [(3, 0, 0), (3, 0, 1), (2, 1, 0), (1, 1, 0)],
                [(2, 1, 1), (1, 1, 1), (2, 0, 0), (1, 0, 0)],
            ],
        )
        pair3 = exchange(far_3, "tensor", 1)
        fetch([(2, 0, 1), (1, 0, 1), (0, 0, 0)], [(0, 1, 0), (0, 1, 1), (0, 0, 1)])
        near3 = chip_sums([(3, 0, 0), (3, 0, 1)], stacked=False)
        far_a = chip_sums([(2, 1, 0), (1, 1, 0)])
        pair_a = exchange(in_turn(far_a, pair3), "tensor", 1)
        third = jnp.stack([add(near3[h], pair3[h]) for h in range(2)])
        relay = lax.ppermute(third, "tensor", by_neighbour)
        across = lax.ppermute(third, "tensor", middle)
        near_a = chip_sums([(2, 0, 0), (1, 0, 0)], stacked=False)
        far_b = chip_sums([(2, 1, 1), (1, 1, 1)])
        pair_b = exchange(in_turn(far_b, pair_a), "tensor", 1)
        second_a = exchange(add(near_a[0], pair_a[0], relay[0]), "tensor", 4)
        first_a = exchange(add(after(near_a[1], across), pair_a[1]), "tensor", 2)
        near_b = chip_sums([(2, 0, 1), (1, 0, 1)], stacked=False)
        far_0 = chip_sums([(0, 1, 0), (0, 1, 1)])
        pair_0 = exchange(in_turn(far_0, pair_b), "tensor", 1)
        second_b = exchange(add(near_b[0], pair_b[0], relay[1]), "tensor", 4)
        first_b = exchange(add(near_b[1], pair_b[1]), "tensor", 2)
        own = chip_sums([(0, 0, 0), (0, 0, 1)], stacked=False)
        early = emit(in_turn(own[0]) + wide(first_a) + wide(second_a) + wide(across[0]))
        hidden = [finish(early, pair_0[0]), finish(own[1], pair_0[1], first_b, second_b, across[1])]
        return jnp.concatenate(give(jnp.concatenate(hidden, axis=1)), axis=1)
    received = []
    for p in range(pairs - 1, -1, -1):
        fetch([(p, 1, 0), (p, 0, 0)])
        from_pair = exchange(chip_sums([(p, 1, 0)])[0], "tensor", 1)
        own = chip_sums([(p, 0, 0)], stacked=False)[0]
        if p:
            received.append(exchange(add(own, from_pair), "tensor", 2 * p))
    return jnp.concatenate(give(finish(own, from_pair, *received)), axis=1)


def solution(mesh):
    in_specs = (
        P(("group", "wide"), "tensor"),
        P("group"),
        P(("group", "wide", "tensor"), None),
        P(("group", "wide", "tensor"), None),
        P("group", None),
        P("group", None),
    )
    out_specs = P(("group", "wide"), "tensor")
    return jax.shard_map(local, mesh=mesh, in_specs=in_specs, out_specs=out_specs, check_vma=False)
```

```python
import functools

import jax
import jax.numpy as jnp
from jax import lax
from jax.experimental import pallas as pl
from jax.experimental.pallas import tpu as pltpu
from jax.sharding import PartitionSpec as P

EPS = 1e-05
LANES = 128
VMEM_LIMIT = 52 * 1024 * 1024


def exchange(value, axis, bit):
    size = lax.axis_size(axis)
    return lax.ppermute(value, axis, [(i, i ^ bit) for i in range(size)])


def after(value, *earlier):
    return lax.optimization_barrier((value, *earlier))[0]


def split_kernel(own_ref, other_ref, gains_ref, out_ref):
    rows, depth = own_ref.shape
    for i, ref in enumerate((own_ref, other_ref)):
        value = ref[...].astype(jnp.float32) * gains_ref[i : i + 1, :]
        high = value.astype(jnp.bfloat16)
        columns = slice(i * depth, (i + 1) * depth)
        out_ref[:rows, columns] = high
        out_ref[rows:, columns] = (value - high.astype(jnp.float32)).astype(jnp.bfloat16)


def split(own, other, gains):
    rows, depth = own.shape
    return pl.pallas_call(
        split_kernel,
        out_shape=jax.ShapeDtypeStruct((2 * rows, 2 * depth), jnp.bfloat16),
        name="split",
    )(own, other, gains)


def cut_copies(groups, lanes, at_ref, gate_ref, up_ref, out_refs, held, in_sems, out_sems):
    weights = (gate_ref, up_ref)
    every = []
    for places, out_ref in zip(groups, out_refs):
        for n, (offset, start) in enumerate(places):
            first = pl.multiple_of((at_ref[0] ^ offset) * at_ref[2] + at_ref[1] + start, LANES)
            for i in range(2):
                k = len(every)
                every.append(
                    (
                        pltpu.make_async_copy(weights[i].at[:, pl.ds(first, lanes)], held.at[k], in_sems.at[k]),
                        pltpu.make_async_copy(held.at[k], out_ref.at[n, i], out_sems.at[k]),
                    )
                )
    return every


def cut_scratch(groups, depth, lanes):
    count = 2 * sum(map(len, groups))
    return [
        pltpu.VMEM((count, depth, lanes), jnp.bfloat16),
        pltpu.SemaphoreType.DMA((count,)),
        pltpu.SemaphoreType.DMA((count,)),
    ]


def cut_kernel(groups, lanes, at_ref, gate_ref, up_ref, *refs):
    every = cut_copies(groups, lanes, at_ref, gate_ref, up_ref, refs[:-3], *refs[-3:])
    for copy_in, _ in every:
        copy_in.start()
    for copy_in, copy_out in every:
        copy_in.wait()
        copy_out.start()
    for _, copy_out in every:
        copy_out.wait()


def cut(at, gate_weight, up_weight, groups, lanes):
    depth = gate_weight.shape[0]
    hbm = pl.BlockSpec(memory_space=pltpu.HBM)
    return pl.pallas_call(
        functools.partial(cut_kernel, groups, lanes),
        in_specs=[pl.BlockSpec(memory_space=pltpu.SMEM), hbm, hbm],
        out_specs=[hbm] * len(groups),
        out_shape=[jax.ShapeDtypeStruct((len(places), 2, depth, lanes), jnp.bfloat16) for places in groups],
        scratch_shapes=cut_scratch(groups, depth, lanes),
        compiler_params=pltpu.CompilerParams(vmem_limit_bytes=VMEM_LIMIT),
        name="cut",
    )(at, gate_weight, up_weight)


def sums_kernel(
    places, lanes, side, stacked, groups, messages, at_ref, partner_ref, x_ref, gate_ref, up_ref, masks_ref, *refs
):
    theirs_refs, refs = refs[:messages], refs[messages:]
    outs = 1 if stacked else len(places)
    out_refs, refs = refs[:outs], refs[outs:]
    cut_refs, refs = refs[: len(groups)], refs[len(groups) :]
    kept, result, in_sems, out_sems = refs[:4]
    depth = gate_ref.shape[0]
    weights = (gate_ref, up_ref)
    firsts = [
        pl.multiple_of((at_ref[0] ^ offset) * at_ref[2] + at_ref[1] + start, LANES) for offset, start, *_ in places
    ]

    def copies_in(n, i):
        return (
            pltpu.make_async_copy(
                weights[i].at[:, pl.ds(firsts[n], lanes)], kept.at[n, i, pl.ds(0, depth)], in_sems.at[n, i, 0]
            ),
            pltpu.make_async_copy(
                theirs_refs[places[n][2]].at[places[n][3], i], kept.at[n, i, pl.ds(depth, depth)], in_sems.at[n, i, 1]
            ),
        )

    def copy_out(n, i):
        out = out_refs[0].at[n, i] if stacked else out_refs[n].at[i]
        return pltpu.make_async_copy(result.at[n, i], out, out_sems.at[n, i])

    every = [(n, i) for n in range(len(places)) for i in range(2)]
    ahead = 3
    for one in every[:ahead]:
        for copy in copies_in(*one):
            copy.start()
    cuts = cut_copies(groups, lanes, partner_ref, gate_ref, up_ref, cut_refs, *refs[4:]) if groups else []
    for copy_in, _ in cuts:
        copy_in.start()
    across = masks_ref.shape[1]
    blocks = 2 * depth // side
    for k, (n, i) in enumerate(every):
        if k + ahead < len(every):
            for copy in copies_in(*every[k + ahead]):
                copy.start()
        if i == 0:
            block = lax.broadcasted_iota(jnp.int32, (across, lanes), 0)
            column = firsts[n] + lax.broadcasted_iota(jnp.int32, (across, lanes), 1)
            spread = ((column >= block * side) & (column < (block + 1) * side)).astype(jnp.bfloat16)
            masks = jnp.dot(masks_ref[...], spread, preferred_element_type=jnp.float32).astype(jnp.bfloat16)
        for copy in copies_in(n, i):
            copy.wait()
        for b in range(blocks):
            rows = slice(b * side, (b + 1) * side)
            kept[n, i, rows, :] = kept[n, i, rows, :] * masks[i * blocks + b : i * blocks + b + 1, :]
        total = jnp.dot(x_ref[...], kept[n, i], preferred_element_type=jnp.float32)
        tokens = result.shape[2]
        if total.shape[0] > tokens:
            total = total[:tokens] + total[tokens:]
        result[n, i] = total.astype(result.dtype)
        copy_out(n, i).start()
    for copy_in, copy_out_cut in cuts:
        copy_in.wait()
        copy_out_cut.start()
    for one in every:
        copy_out(*one).wait()
    for _, copy_out_cut in cuts:
        copy_out_cut.wait()


def sums(at, x, gate_weight, up_weight, theirs, masks, side, places, lanes, dtype, stacked, partner, groups, tokens):
    depth = gate_weight.shape[0]
    count = len(places)
    vmem = pl.BlockSpec(memory_space=pltpu.VMEM)
    hbm = pl.BlockSpec(memory_space=pltpu.HBM)
    return pl.pallas_call(
        functools.partial(sums_kernel, places, lanes, side, stacked, groups, len(theirs)),
        in_specs=[pl.BlockSpec(memory_space=pltpu.SMEM)] * 2 + [vmem, hbm, hbm, vmem] + [hbm] * len(theirs),
        out_specs=[hbm] * ((1 if stacked else count) + len(groups)),
        out_shape=(
            [jax.ShapeDtypeStruct((count, 2, tokens, lanes), dtype)]
            if stacked
            else [jax.ShapeDtypeStruct((2, tokens, lanes), dtype)] * count
        )
        + [jax.ShapeDtypeStruct((len(units), 2, depth, lanes), jnp.bfloat16) for units in groups],
        scratch_shapes=[
            pltpu.VMEM((count, 2, 2 * depth, lanes), jnp.bfloat16),
            pltpu.VMEM((count, 2, tokens, lanes), dtype),
            pltpu.SemaphoreType.DMA((count, 2, 2)),
            pltpu.SemaphoreType.DMA((count, 2)),
        ]
        + (cut_scratch(groups, depth, lanes) if groups else []),
        compiler_params=pltpu.CompilerParams(vmem_limit_bytes=VMEM_LIMIT),
        name="sums",
    )(at, partner, x, gate_weight, up_weight, masks, *theirs)


def local(tokens, gain, gate_weight, up_weight, gate_mask, up_mask):
    shards = lax.axis_size("tensor")
    shard = lax.axis_index("tensor")
    half = lax.axis_index("wide")
    depth, width = gate_weight.shape
    features = gain.shape[0]
    rows = tokens.shape[0]
    per_shard = width // shards
    per_core = per_shard // 2
    pairs = shards // 2

    mine = jnp.stack([shard, half * per_core, per_shard]).astype(jnp.int32)
    partners = jnp.stack([shard, (1 - half) * per_core, per_shard]).astype(jnp.int32)
    side = features // gate_mask.shape[0]
    first_rows = [half * (features // 2) + shard * depth, (1 - half) * (features // 2) + shard * depth]
    lanes = per_core // 2 if pairs == 4 else per_core
    theirs, pair, far = {}, {}, {}

    def place(unit):
        p, y, h = unit
        return (2 * p + y, h * lanes)

    latest = []

    def in_turn(value, *more):
        return after(value, *latest, *more)

    def emit(value):
        latest[:] = [value]
        return value

    def in_place(groups):
        return tuple(tuple(map(place, units)) for units in groups)

    def swap(groups, values):
        for units, value in zip(groups, values):
            value = exchange(value, "wide", 1)
            for n, unit in enumerate(units):
                theirs[unit] = (value, n)

    def fetch(*groups):
        values = cut(in_turn(partners), gate_weight, up_weight, in_place(groups), lanes)
        emit(values[0])
        swap(groups, values)

    if pairs == 4:
        fetch([(3, 1, 0), (3, 1, 1)])
    raw = []
    for flip in range(2):
        moves = []
        for w in range(2):
            for t in range(shards):
                moves.append((((t % 2) ^ flip) * shards + w * pairs + t // 2, w * shards + t))
        piece = lax.dynamic_slice_in_dim(tokens, (half ^ flip) * depth, depth, 1)
        raw.append(lax.ppermute(piece, ("wide", "tensor"), moves))
    values = tokens.astype(jnp.float32)
    squares = jnp.sum(values * values, axis=-1).reshape(1, rows)
    squares_other = exchange(squares, "wide", 1)
    squares = jnp.where(
        half == 0,
        jnp.concatenate([squares, squares_other], axis=0),
        jnp.concatenate([squares_other, squares], axis=0),
    )
    squares = squares + exchange(squares, "tensor", 1)
    raw = jnp.where(shard % 2 == 1, jnp.concatenate(raw[::-1]), jnp.concatenate(raw))
    masks = jnp.concatenate(
        [
            lax.dynamic_slice_in_dim(mask, r // side, depth // side, 0)
            for mask in (gate_mask, up_mask)
            for r in first_rows
        ]
    ).astype(jnp.bfloat16)
    gains = jnp.stack([lax.dynamic_slice_in_dim(gain, r, depth, 0) for r in first_rows])
    raw_other = exchange(raw, "wide", 1)

    def normalise(start):
        total, bit = after(squares, start), 2
        while bit < shards:
            total = total + exchange(total, "tensor", bit)
            bit *= 2
        scales = lax.rsqrt(total / features + EPS).reshape(2 * rows, 1)
        parts = [
            (part.astype(jnp.float32) * scales * gains[i : i + 1]).astype(jnp.bfloat16)
            for i, part in enumerate((raw, raw_other))
        ]
        return jnp.concatenate(parts, axis=1), scales

    def chip_sums(x, units, stacked=True, groups=()):
        messages = []
        for unit in units:
            if not any(theirs[unit][0] is message for message in messages):
                messages.append(theirs[unit][0])
        places = tuple(
            (*place(unit), [theirs[unit][0] is m for m in messages].index(True), theirs[unit][1]) for unit in units
        )
        dtype = jnp.bfloat16 if stacked else jnp.float32
        values = sums(
            mine, in_turn(x), gate_weight, up_weight, messages, masks, side, places, lanes, dtype, stacked,
            partners, in_place(groups), 2 * rows
        )
        emit(values[0])
        outs = 1 if stacked else len(units)
        swap(groups, values[outs:])
        return values[0] if stacked else values

    def finish(own, *terms):
        total = in_turn(own)
        for term in terms:
            total = total + wide(term)
        return (jax.nn.silu(total[0]) * total[1]).astype(jnp.bfloat16)

    def add(own, *terms):
        total = in_turn(own)
        for term in terms:
            total = total + wide(term)
        return emit(total.astype(jnp.bfloat16))

    def give(hidden):
        keep = lax.dynamic_slice_in_dim(hidden, half * rows, rows, 0)
        got = exchange(lax.dynamic_slice_in_dim(hidden, (1 - half) * rows, rows, 0), "wide", 1)
        return jnp.where(half == 0, keep, got), jnp.where(half == 0, got, keep)

    wide = lambda value: value.astype(jnp.float32)

    if pairs == 4:
        tensor_pairs = lambda moves: [(2 * i + y, 2 * j + y) for i, j in moves for y in range(2)]
        by_neighbour = tensor_pairs(((0, 1), (3, 2)))
        middle = tensor_pairs(((1, 2), (2, 1)))

        latest.extend([masks, gains])
        unscaled = split(after(raw, squares), raw_other, gains)
        far_3 = chip_sums(
            unscaled,
            [(3, 1, 0), (3, 1, 1)],
            groups=[
                [(3, 0, 0), (3, 0, 1), (2, 1, 0), (1, 1, 0)],
                [(2, 1, 1), (1, 1, 1), (2, 0, 0), (1, 0, 0)],
            ],
        )
        pair3 = exchange(far_3, "tensor", 1)
        normed, scales = normalise(far_3)
        fetch([(2, 0, 1), (1, 0, 1), (0, 0, 0)], [(0, 1, 0), (0, 1, 1), (0, 0, 1)])
        near3 = chip_sums(unscaled, [(3, 0, 0), (3, 0, 1)], stacked=False)
        far_a = chip_sums(unscaled, [(2, 1, 0), (1, 1, 0)])
        pair_a = exchange(in_turn(far_a, pair3), "tensor", 1)
        third = jnp.stack([add(near3[h], pair3[h]) for h in range(2)])
        relay = lax.ppermute(third, "tensor", by_neighbour)
        across = lax.ppermute(third, "tensor", middle)
        near_a = chip_sums(normed, [(2, 0, 0), (1, 0, 0)], stacked=False)
        far_b = chip_sums(normed, [(2, 1, 1), (1, 1, 1)])
        pair_b = exchange(in_turn(far_b, pair_a), "tensor", 1)
        second_a = exchange(add(near_a[0], (wide(pair_a[0]) + wide(relay[0])) * scales), "tensor", 4)
        first_a = exchange(add(after(near_a[1], across), wide(pair_a[1]) * scales), "tensor", 2)
        near_b = chip_sums(normed, [(2, 0, 1), (1, 0, 1)], stacked=False)
        far_0 = chip_sums(normed, [(0, 1, 0), (0, 1, 1)])
        pair_0 = exchange(in_turn(far_0, pair_b), "tensor", 1)
        second_b = exchange(add(near_b[0], pair_b[0], wide(relay[1]) * scales), "tensor", 4)
        first_b = exchange(add(near_b[1], pair_b[1]), "tensor", 2)
        own = chip_sums(normed, [(0, 0, 0), (0, 0, 1)], stacked=False)
        early = emit(in_turn(own[0]) + wide(first_a) + wide(second_a) + wide(across[0]) * scales)
        hidden = [finish(early, pair_0[0]), finish(own[1], pair_0[1], first_b, second_b, wide(across[1]) * scales)]
        return jnp.concatenate(give(jnp.concatenate(hidden, axis=1)), axis=1)
    received = []
    normed, _ = normalise(squares)
    for p in range(pairs - 1, -1, -1):
        fetch([(p, 1, 0), (p, 0, 0)])
        from_pair = exchange(chip_sums(normed, [(p, 1, 0)])[0], "tensor", 1)
        own = chip_sums(normed, [(p, 0, 0)], stacked=False)[0]
        if p:
            received.append(exchange(add(own, from_pair), "tensor", 2 * p))
    return jnp.concatenate(give(finish(own, from_pair, *received)), axis=1)


def solution(mesh):
    in_specs = (
        P(("group", "wide"), "tensor"),
        P("group"),
        P(("group", "wide", "tensor"), None),
        P(("group", "wide", "tensor"), None),
        P("group", None),
        P("group", None),
    )
    out_specs = P(("group", "wide"), "tensor")
    return jax.shard_map(local, mesh=mesh, in_specs=in_specs, out_specs=out_specs, check_vma=False)
```

```python
import functools

import jax
import jax.numpy as jnp
from jax import lax
from jax.experimental import pallas as pl
from jax.experimental.pallas import tpu as pltpu
from jax.sharding import PartitionSpec as P

EPS = 1e-05
LANES = 128
VMEM_LIMIT = 49 * 1024 * 1024


def exchange(value, axis, bit):
    size = lax.axis_size(axis)
    return lax.ppermute(value, axis, [(i, i ^ bit) for i in range(size)])


def after(value, *earlier):
    return lax.optimization_barrier((value, *earlier))[0]


def split(own, other, gains):
    values = [part.astype(jnp.float32) * gains[i : i + 1] for i, part in enumerate((own, other))]
    value = jnp.concatenate(values, axis=1)
    high = lax.reduce_precision(value, exponent_bits=8, mantissa_bits=7)
    return jnp.concatenate([high, value - high], axis=0).astype(jnp.bfloat16)


def cut_copies(groups, lanes, at_ref, gate_ref, up_ref, out_refs, held, in_sems, out_sems):
    weights = (gate_ref, up_ref)
    every = []
    for places, out_ref in zip(groups, out_refs):
        for n, (offset, start) in enumerate(places):
            first = pl.multiple_of((at_ref[0] ^ offset) * at_ref[2] + at_ref[1] + start, LANES)
            for i in range(2):
                k = len(every)
                every.append(
                    (
                        pltpu.make_async_copy(weights[i].at[:, pl.ds(first, lanes)], held.at[k], in_sems.at[k]),
                        pltpu.make_async_copy(held.at[k], out_ref.at[n, i], out_sems.at[k]),
                    )
                )
    return every


def cut_scratch(groups, depth, lanes):
    count = 2 * sum(map(len, groups))
    return [
        pltpu.VMEM((count, depth, lanes), jnp.bfloat16),
        pltpu.SemaphoreType.DMA((count,)),
        pltpu.SemaphoreType.DMA((count,)),
    ]


def cut_kernel(groups, lanes, at_ref, gate_ref, up_ref, *refs):
    every = cut_copies(groups, lanes, at_ref, gate_ref, up_ref, refs[:-3], *refs[-3:])
    for copy_in, _ in every:
        copy_in.start()
    for copy_in, copy_out in every:
        copy_in.wait()
        copy_out.start()
    for _, copy_out in every:
        copy_out.wait()


def cut(at, gate_weight, up_weight, groups, lanes):
    depth = gate_weight.shape[0]
    hbm = pl.BlockSpec(memory_space=pltpu.HBM)
    return pl.pallas_call(
        functools.partial(cut_kernel, groups, lanes),
        in_specs=[pl.BlockSpec(memory_space=pltpu.SMEM), hbm, hbm],
        out_specs=[hbm] * len(groups),
        out_shape=[jax.ShapeDtypeStruct((len(places), 2, depth, lanes), jnp.bfloat16) for places in groups],
        scratch_shapes=cut_scratch(groups, depth, lanes),
        compiler_params=pltpu.CompilerParams(vmem_limit_bytes=VMEM_LIMIT),
        name="cut",
    )(at, gate_weight, up_weight)


def sums_kernel(
    places, lanes, side, stacked, groups, messages, at_ref, partner_ref, x_ref, gate_ref, up_ref, masks_ref, *refs
):
    theirs_refs, refs = refs[:messages], refs[messages:]
    outs = 1 if stacked else len(places)
    out_refs, refs = refs[:outs], refs[outs:]
    cut_refs, refs = refs[: len(groups)], refs[len(groups) :]
    kept, result, in_sems, out_sems = refs[:4]
    depth = gate_ref.shape[0]
    weights = (gate_ref, up_ref)
    firsts = [
        pl.multiple_of((at_ref[0] ^ offset) * at_ref[2] + at_ref[1] + start, LANES) for offset, start, *_ in places
    ]

    def copies_in(n, i):
        return (
            pltpu.make_async_copy(
                weights[i].at[:, pl.ds(firsts[n], lanes)], kept.at[n, i, pl.ds(0, depth)], in_sems.at[n, i, 0]
            ),
            pltpu.make_async_copy(
                theirs_refs[places[n][2]].at[places[n][3], i], kept.at[n, i, pl.ds(depth, depth)], in_sems.at[n, i, 1]
            ),
        )

    def copy_out(n, i):
        out = out_refs[0].at[n, i] if stacked else out_refs[n].at[i]
        return pltpu.make_async_copy(result.at[n, i], out, out_sems.at[n, i])

    every = [(n, i) for n in range(len(places)) for i in range(2)]
    ahead = 3
    for one in every[:ahead]:
        for copy in copies_in(*one):
            copy.start()
    cuts = cut_copies(groups, lanes, partner_ref, gate_ref, up_ref, cut_refs, *refs[4:]) if groups else []
    for copy_in, _ in cuts:
        copy_in.start()
    across = masks_ref.shape[1]
    blocks = 2 * depth // side
    for k, (n, i) in enumerate(every):
        if k + ahead < len(every):
            for copy in copies_in(*every[k + ahead]):
                copy.start()
        if i == 0:
            block = lax.broadcasted_iota(jnp.int32, (across, lanes), 0)
            column = firsts[n] + lax.broadcasted_iota(jnp.int32, (across, lanes), 1)
            spread = ((column >= block * side) & (column < (block + 1) * side)).astype(jnp.bfloat16)
            masks = jnp.dot(masks_ref[...], spread, preferred_element_type=jnp.float32).astype(jnp.bfloat16)
        for copy in copies_in(n, i):
            copy.wait()
        for b in range(blocks):
            rows = slice(b * side, (b + 1) * side)
            kept[n, i, rows, :] = kept[n, i, rows, :] * masks[i * blocks + b : i * blocks + b + 1, :]
        total = jnp.dot(x_ref[...], kept[n, i], preferred_element_type=jnp.float32)
        tokens = result.shape[2]
        if total.shape[0] > tokens:
            total = total[:tokens] + total[tokens:]
        result[n, i] = total.astype(result.dtype)
        copy_out(n, i).start()
    for copy_in, copy_out_cut in cuts:
        copy_in.wait()
        copy_out_cut.start()
    for one in every:
        copy_out(*one).wait()
    for _, copy_out_cut in cuts:
        copy_out_cut.wait()


def sums(at, x, gate_weight, up_weight, theirs, masks, side, places, lanes, dtype, stacked, partner, groups, tokens):
    depth = gate_weight.shape[0]
    count = len(places)
    vmem = pl.BlockSpec(memory_space=pltpu.VMEM)
    hbm = pl.BlockSpec(memory_space=pltpu.HBM)
    return pl.pallas_call(
        functools.partial(sums_kernel, places, lanes, side, stacked, groups, len(theirs)),
        in_specs=[pl.BlockSpec(memory_space=pltpu.SMEM)] * 2 + [vmem, hbm, hbm, vmem] + [hbm] * len(theirs),
        out_specs=[hbm] * ((1 if stacked else count) + len(groups)),
        out_shape=(
            [jax.ShapeDtypeStruct((count, 2, tokens, lanes), dtype)]
            if stacked
            else [jax.ShapeDtypeStruct((2, tokens, lanes), dtype)] * count
        )
        + [jax.ShapeDtypeStruct((len(units), 2, depth, lanes), jnp.bfloat16) for units in groups],
        scratch_shapes=[
            pltpu.VMEM((count, 2, 2 * depth, lanes), jnp.bfloat16),
            pltpu.VMEM((count, 2, tokens, lanes), dtype),
            pltpu.SemaphoreType.DMA((count, 2, 2)),
            pltpu.SemaphoreType.DMA((count, 2)),
        ]
        + (cut_scratch(groups, depth, lanes) if groups else []),
        compiler_params=pltpu.CompilerParams(vmem_limit_bytes=VMEM_LIMIT),
        name="sums",
    )(at, partner, x, gate_weight, up_weight, masks, *theirs)


def local(tokens, gain, gate_weight, up_weight, gate_mask, up_mask):
    shards = lax.axis_size("tensor")
    shard = lax.axis_index("tensor")
    half = lax.axis_index("wide")
    depth, width = gate_weight.shape
    features = gain.shape[0]
    rows = tokens.shape[0]
    per_shard = width // shards
    per_core = per_shard // 2
    pairs = shards // 2

    mine = jnp.stack([shard, half * per_core, per_shard]).astype(jnp.int32)
    partners = jnp.stack([shard, (1 - half) * per_core, per_shard]).astype(jnp.int32)
    side = features // gate_mask.shape[0]
    first_rows = [half * (features // 2) + shard * depth, (1 - half) * (features // 2) + shard * depth]
    lanes = per_core // 2 if pairs == 4 else per_core
    theirs, pair, far = {}, {}, {}

    def place(unit):
        p, y, h = unit
        return (2 * p + y, h * lanes)

    latest = []

    def in_turn(value, *more):
        return after(value, *latest, *more)

    def emit(value):
        latest[:] = [value]
        return value

    def in_place(groups):
        return tuple(tuple(map(place, units)) for units in groups)

    def swap(groups, values):
        for units, value in zip(groups, values):
            value = exchange(value, "wide", 1)
            for n, unit in enumerate(units):
                theirs[unit] = (value, n)

    def fetch(*groups):
        values = cut(in_turn(partners), gate_weight, up_weight, in_place(groups), lanes)
        emit(values[0])
        swap(groups, values)

    if pairs == 4:
        fetch([(3, 1, 0), (3, 1, 1)])
    raw = []
    for flip in range(2):
        moves = []
        for w in range(2):
            for t in range(shards):
                moves.append((((t % 2) ^ flip) * shards + w * pairs + t // 2, w * shards + t))
        piece = lax.dynamic_slice_in_dim(tokens, (half ^ flip) * depth, depth, 1)
        raw.append(lax.ppermute(piece, ("wide", "tensor"), moves))
    values = tokens.astype(jnp.float32)
    squares = jnp.sum(values * values, axis=-1).reshape(1, rows)
    squares = squares + exchange(squares, "tensor", 1)
    squares_other = exchange(squares, "wide", 1)
    squares = jnp.where(
        half == 0,
        jnp.concatenate([squares, squares_other], axis=0),
        jnp.concatenate([squares_other, squares], axis=0),
    )
    raw = jnp.where(shard % 2 == 1, jnp.concatenate(raw[::-1]), jnp.concatenate(raw))
    masks = jnp.concatenate(
        [
            lax.dynamic_slice_in_dim(mask, r // side, depth // side, 0)
            for mask in (gate_mask, up_mask)
            for r in first_rows
        ]
    ).astype(jnp.bfloat16)
    gains = jnp.stack([lax.dynamic_slice_in_dim(gain, r, depth, 0) for r in first_rows])
    raw_other = exchange(raw, "wide", 1)

    def normalise(start):
        total, bit = after(squares, start), 2
        while bit < shards:
            total = total + exchange(total, "tensor", bit)
            bit *= 2
        scales = lax.rsqrt(total / features + EPS).reshape(2 * rows, 1)
        parts = [
            (part.astype(jnp.float32) * scales * gains[i : i + 1]).astype(jnp.bfloat16)
            for i, part in enumerate((raw, raw_other))
        ]
        return jnp.concatenate(parts, axis=1), scales

    def chip_sums(x, units, stacked=True, groups=()):
        messages = []
        for unit in units:
            if not any(theirs[unit][0] is message for message in messages):
                messages.append(theirs[unit][0])
        places = tuple(
            (*place(unit), [theirs[unit][0] is m for m in messages].index(True), theirs[unit][1]) for unit in units
        )
        dtype = jnp.bfloat16 if stacked else jnp.float32
        values = sums(
            mine, in_turn(x), gate_weight, up_weight, messages, masks, side, places, lanes, dtype, stacked,
            partners, in_place(groups), 2 * rows
        )
        emit(values[0])
        outs = 1 if stacked else len(units)
        swap(groups, values[outs:])
        return values[0] if stacked else values

    def finish(own, *terms):
        total = in_turn(own)
        for term in terms:
            total = total + wide(term)
        return (jax.nn.silu(total[0]) * total[1]).astype(jnp.bfloat16)

    def add(own, *terms):
        total = in_turn(own)
        for term in terms:
            total = total + wide(term)
        return emit(total.astype(jnp.bfloat16))

    def give(hidden):
        keep = lax.dynamic_slice_in_dim(hidden, half * rows, rows, 0)
        got = exchange(lax.dynamic_slice_in_dim(hidden, (1 - half) * rows, rows, 0), "wide", 1)
        return jnp.where(half == 0, keep, got), jnp.where(half == 0, got, keep)

    wide = lambda value: value.astype(jnp.float32)

    if pairs == 4:
        tensor_pairs = lambda moves: [(2 * i + y, 2 * j + y) for i, j in moves for y in range(2)]
        by_neighbour = tensor_pairs(((0, 1), (3, 2)))
        middle = tensor_pairs(((1, 2), (2, 1)))

        latest.extend([masks, gains])
        unscaled = split(after(raw, squares), raw_other, gains)
        far_3 = chip_sums(
            unscaled,
            [(3, 1, 0), (3, 1, 1)],
            groups=[
                [(3, 0, 0), (3, 0, 1), (2, 1, 0), (1, 1, 0)],
                [(2, 1, 1), (1, 1, 1), (2, 0, 0), (1, 0, 0)],
            ],
        )
        pair3 = exchange(far_3, "tensor", 1)
        normed, scales = normalise(far_3)
        fetch([(2, 0, 1), (1, 0, 1), (0, 0, 0)], [(0, 1, 0), (0, 1, 1), (0, 0, 1)])
        near3 = chip_sums(unscaled, [(3, 0, 0), (3, 0, 1)], stacked=False)
        far_a = chip_sums(unscaled, [(2, 1, 0), (1, 1, 0)])
        pair_a = exchange(in_turn(far_a, pair3), "tensor", 1)
        third = jnp.stack([add(near3[h], pair3[h]) for h in range(2)])
        relay = lax.ppermute(third, "tensor", by_neighbour)
        across = lax.ppermute(third, "tensor", middle)
        near_a = chip_sums(normed, [(2, 0, 0), (1, 0, 0)], stacked=False)
        far_b = chip_sums(normed, [(2, 1, 1), (1, 1, 1)])
        pair_b = exchange(in_turn(far_b, pair_a), "tensor", 1)
        second_a = exchange(add(near_a[0], (wide(pair_a[0]) + wide(relay[0])) * scales), "tensor", 4)
        first_a = exchange(add(after(near_a[1], across), wide(pair_a[1]) * scales), "tensor", 2)
        near_b = chip_sums(normed, [(2, 0, 1), (1, 0, 1)], stacked=False)
        far_0 = chip_sums(normed, [(0, 1, 0), (0, 1, 1)])
        pair_0 = exchange(in_turn(far_0, pair_b), "tensor", 1)
        second_b = exchange(add(near_b[0], pair_b[0], wide(relay[1]) * scales), "tensor", 4)
        first_b = exchange(add(near_b[1], pair_b[1]), "tensor", 2)
        own = chip_sums(normed, [(0, 0, 0), (0, 0, 1)], stacked=False)
        early = emit(in_turn(own[0]) + wide(first_a) + wide(across[0]) * scales)
        hidden = [finish(early, pair_0[0], second_a), finish(own[1], pair_0[1], first_b, second_b, wide(across[1]) * scales)]
        return jnp.concatenate(give(jnp.concatenate(hidden, axis=1)), axis=1)
    received = []
    normed, _ = normalise(squares)
    for p in range(pairs - 1, -1, -1):
        fetch([(p, 1, 0), (p, 0, 0)])
        from_pair = exchange(chip_sums(normed, [(p, 1, 0)])[0], "tensor", 1)
        own = chip_sums(normed, [(p, 0, 0)], stacked=False)[0]
        if p:
            received.append(exchange(add(own, from_pair), "tensor", 2 * p))
    return jnp.concatenate(give(finish(own, from_pair, *received)), axis=1)


def solution(mesh):
    in_specs = (
        P(("group", "wide"), "tensor"),
        P("group"),
        P(("group", "wide", "tensor"), None),
        P(("group", "wide", "tensor"), None),
        P("group", None),
        P("group", None),
    )
    out_specs = P(("group", "wide"), "tensor")
    return jax.shard_map(local, mesh=mesh, in_specs=in_specs, out_specs=out_specs, check_vma=False)
```
